32 devices in a mesh: groups: 2 (over y), expert: 4 (over z), cuts: 4 (over x, core).
Axes of the slice: x: 2, y: 2, z: 4, core: 2. Of those that a mesh axis runs over, the one named last changes fastest.
Arguments:
- tokens: bfloat16 [256, 4096], P(('groups', 'expert', 'cuts')), parts along dimension 0, may hold values from -30 to 30
- router_weight: bfloat16 [4096, 4], replicated, may hold values from -0.09375 to 0.09375
- gate_weight: bfloat16 [4, 4096, 8192], P('expert', None, 'cuts'), may hold values from -0.09375 to 0.09375
- up_weight: bfloat16 [4, 4096, 8192], P('expert', None, 'cuts'), may hold values from -0.09375 to 0.09375
- down_weight: bfloat16 [4, 8192, 4096], P('expert', 'cuts'), may hold values from -0.0625 to 0.0625
- expert_ids: int32 [256, 2], P(('groups', 'expert', 'cuts')), parts along dimension 0, may hold values from 0 to 3, all different within a row; in each aligned block of 8 rows (0 to 7, 8 to 15, ...) at most 4 rows name the same one
Outputs:
- mixed: bfloat16 [256, 4096], P(('groups', 'expert', 'cuts')), parts along dimension 0
- router_stats: float32 [4], P('groups'), parts along dimension 0
The draws below stay inside these ranges and needn't reach their ends.
There are 2 independent parts, one for each index of `groups`. The reference program is written for one: setup_inputs(seed, part) draws one part's arguments, and reference() takes and returns one part's arrays. A program takes and returns all parts, laid end to end along the dimension named above; an argument that names none is the same for every part. Nothing has to cross between parts.
Inputs may be any that keep to these rules, and one draw needn't show every extreme that they name: `expert_ids`: each row names 2 different experts; among the 8 rows of one device (aligned blocks of rows) no expert is named by more than 4 rows, and in some blocks one expert is named by exactly 4 rows.
All inputs are finite; a program needn't handle non-finite values.
Results may differ from the reference program's by a relative error of at most 0.0058.
Values may be sent and summed in bfloat16 or wider, within the bound.
A program may use at most 128 MiB of HBM per device.

```python
import math
import jax
import jax.numpy as jnp
import numpy as np
from jax import lax

D = 4096
FF = 8192
TOPK = 2
R_DEV = 8
CAP = 4
EXPERTS = 4
ROWS = 128


def draw_tokens(key, part):
    key = jax.random.fold_in(key, 11)
    first, second = jax.random.split(key, 2)
    ramp = jnp.arange(ROWS, dtype=jnp.float32) / (ROWS - 1)
    base = jnp.clip(jax.random.normal(first, (ROWS, D), jnp.float32), -5.0, 5.0)
    row_scale = 0.3 * jnp.power(10.0, ramp)
    col_scale = jnp.exp(jax.random.uniform(second, (D,), jnp.float32, jnp.log(0.5), jnp.log(2.0)))
    return (base * row_scale[:, None] * col_scale[None, :]).astype(jnp.bfloat16)


def block_scale(rng, extent, cuts, least, largest):
    level = 1.0
    for dim, shards_of in cuts:
        steps = jax.random.uniform(jax.random.fold_in(jax.random.fold_in(rng, 6), dim), (shards_of,), jnp.float32, least / len(cuts), largest / len(cuts))
        level = level * jnp.repeat(jnp.exp(steps), extent[dim] // shards_of).reshape((-1,) + (1,) * (len(extent) - 1 - dim))
    return level


def assign_block(stream_key, own, number, rows, count, top, reach, slope):
    ranking = jax.random.permutation(stream_key, count)
    packed, ordinary = shares(count, rows * top, reach, slope, True), shares(count, rows * top, reach, slope, False)
    places = jnp.arange(count)

    def named(lengths, turn):
        used = int((lengths > 0).sum())
        fixed = max(1, used // 4)
        passed = fixed + (places - fixed + turn * (used - fixed)) % max(1, count - fixed)
        return jnp.zeros((count,), jnp.int32).at[ranking[jnp.where(places < fixed, places, passed)]].set(jnp.asarray(lengths, jnp.int32))

    lengths = jnp.where(number % 4 == 0, named(packed, number // 4), named(ordinary, number - number // 4 - 1))
    mixed = jax.random.permutation(jax.random.fold_in(own, 3), count)
    giver, sink = mixed[0:count // 2 * 2:2], mixed[1:count // 2 * 2:2]
    slack = jnp.minimum(lengths[giver] - 1, reach - lengths[sink]) // 2
    slack = jnp.where((giver == ranking[0]) | (sink == ranking[0]) | (lengths[sink] == 0), 0, jnp.maximum(slack, 0))
    passed = jax.random.randint(jax.random.fold_in(own, 4), (count // 2,), 0, 1 << 20) % (slack + 1)
    lengths = lengths.at[giver].add(-passed).at[sink].add(passed)
    items = jnp.searchsorted(jnp.cumsum(lengths), jnp.arange(rows * top), side="right").astype(jnp.int32)
    listing = items.reshape(top, rows).T
    listing = listing[jax.random.permutation(jax.random.fold_in(own, 1), rows)]
    turn = jax.random.randint(jax.random.fold_in(own, 2), (rows, 1), 0, top)
    return jnp.take_along_axis(listing, (jnp.arange(top)[None, :] + turn) % top, axis=1)


def shares(number_of, total, bound, lean, full):
    loads = [(1 << 20) // math.isqrt(standing ** lean) + 1 for standing in range(1, number_of + 1)]
    largest = bound if full else min(bound, max(-(-total // number_of), total * loads[0] // sum(loads)))
    least = 1 if total - largest >= number_of - 1 else 0
    counts, rest = [largest] + [least] * (number_of - 1), total - largest - least * (number_of - 1)
    while rest > 0:
        free = [i for i in range(1, number_of) if counts[i] < largest] or [i for i in range(1, number_of) if counts[i] < bound]
        pool, budget = sum([loads[i] for i in free]), rest
        for i in free:
            addition = min(bound - counts[i], max(1, budget * loads[i] // pool), rest)
            counts[i] = counts[i] + addition
            rest = rest - addition
    return np.array(counts)


def noise(stream_key, extent, scale, limit, cuts=(), kind=jnp.bfloat16):
    drawn = scale * jax.random.normal(stream_key, extent, jnp.float32)
    if cuts:
        drawn = drawn * block_scale(stream_key, extent, cuts, -0.22, 0.18)
    return jnp.clip(drawn, -limit, limit).astype(kind)


def setup_inputs(seed: int = 0, part: int = 0) -> dict:
    streams_of = jax.random.split(jax.random.key(seed), 7)
    part_splits = jax.random.split(jax.random.fold_in(streams_of[6], part), 7)
    tokens = draw_tokens(jax.random.fold_in(jax.random.fold_in(streams_of[6], part), 71), part)
    router_weight = noise(streams_of[1], (D, EXPERTS), D ** -0.5, 0.09375)
    gate_weight = noise(streams_of[2], (EXPERTS, D, FF), D ** -0.5, 0.09375, ((0, 4), (2, 4)))
    up_weight = noise(streams_of[3], (EXPERTS, D, FF), D ** -0.5, 0.09375, ((0, 4), (2, 4)))
    down_weight = noise(streams_of[4], (EXPERTS, FF, D), FF ** -0.5, 0.0625, ((0, 4), (1, 4)))
    expert_ids_keys = jax.random.split(jax.random.fold_in(part_splits[5], 1), ROWS // R_DEV)
    expert_ids_turns = jax.random.permutation(jax.random.fold_in(part_splits[5], 3), ROWS // R_DEV)
    expert_ids = jax.vmap(lambda own, number: assign_block(jax.random.fold_in(part_splits[5], 2), own, number, R_DEV, EXPERTS, TOPK, CAP, 2))(expert_ids_keys, expert_ids_turns).reshape((ROWS, TOPK))
    return dict(tokens=tokens, router_weight=router_weight, gate_weight=gate_weight, up_weight=up_weight, down_weight=down_weight, expert_ids=expert_ids)


def reference(tokens, router_weight, gate_weight, up_weight, down_weight, expert_ids):
    logits = jnp.dot(tokens, router_weight, preferred_element_type=jnp.float32)
    exps = jnp.exp(logits)
    total = jnp.sum(exps, axis=1, keepdims=True)
    probs = exps / total
    log_total = jnp.log(total[:, 0])
    labels = jnp.arange(EXPERTS, dtype=jnp.int32)
    picks = (expert_ids[:, :, None] == labels[None, None, :]).astype(jnp.int32)
    member = jnp.sum(picks, axis=1)
    z_loss = jnp.mean(log_total * log_total)
    importance = jnp.mean(probs, axis=0)
    load = jnp.sum(member, axis=0).astype(jnp.float32) / (ROWS * TOPK)
    balance = EXPERTS * jnp.sum(importance * load)
    router_stats = jnp.stack([z_loss, balance])
    chosen = jnp.sum(picks.astype(jnp.float32) * probs[:, None, :], axis=2)
    combine = chosen / jnp.sum(chosen, axis=1, keepdims=True)
    blocks = ROWS // R_DEV
    member_blocks = member.reshape(blocks, R_DEV, EXPERTS)
    position = jnp.cumsum(member_blocks, axis=1) - member_blocks
    slot_labels = jnp.arange(CAP, dtype=jnp.int32)
    select = ((member_blocks[:, :, :, None] > 0) & (position[:, :, :, None] == slot_labels)).astype(jnp.float32)
    token_blocks = tokens.reshape(blocks, R_DEV, D).astype(jnp.float32)

    def one_expert(index):
        chooser = select[:, :, index, :]
        gathered = jnp.einsum("brj,brd->bjd", chooser, token_blocks).reshape(blocks * CAP, D).astype(jnp.bfloat16)
        gate = jnp.dot(gathered, gate_weight[index], preferred_element_type=jnp.float32)
        upper = jnp.dot(gathered, up_weight[index], preferred_element_type=jnp.float32)
        hidden = (jax.nn.silu(gate) * upper).astype(jnp.bfloat16)
        return jnp.dot(hidden, down_weight[index], preferred_element_type=jnp.float32).astype(jnp.bfloat16)

    outputs = lax.map(one_expert, jnp.arange(EXPERTS, dtype=jnp.int32))
    outputs = outputs.reshape(EXPERTS, blocks, CAP, D)
    position_rows = position.reshape(ROWS, EXPERTS)
    slot_of = jnp.sum(picks * position_rows[:, None, :], axis=2).astype(jnp.int32)
    block_of = (jnp.arange(ROWS, dtype=jnp.int32) // R_DEV)[:, None]
    gathered_out = outputs[expert_ids, block_of, slot_of]
    mixed = jnp.sum(combine[:, :, None] * gathered_out.astype(jnp.float32), axis=1).astype(jnp.bfloat16)
    return mixed, router_stats
```

```python
import functools

import jax
import jax.numpy as jnp
from jax import lax
from jax.experimental import pallas as pl
from jax.experimental.pallas import tpu as pltpu
from jax.sharding import PartitionSpec as P

MESH = pl.DeviceIdType.MESH
PACK = 16


def remote(src, dst, send, recv, axis, peer):
    return pltpu.make_async_remote_copy(
        src_ref=src,
        dst_ref=dst,
        send_sem=send,
        recv_sem=recv,
        device_id={axis: peer},
        device_id_type=MESH,
    )


def fold(rows, parts):
    lanes = rows.shape[1] // parts
    return jnp.concatenate([rows[:, q * lanes : (q + 1) * lanes] for q in range(parts)], axis=0)


def kernel(
    dims,
    tokens_ref,
    router_ref,
    ids_ref,
    gate_hbm,
    up_hbm,
    down_hbm,
    mixed_ref,
    stats_ref,
    w_gate,
    w_up,
    w_down,
    outbox,
    inbox,
    block,
    hidden,
    partial,
    sums_in,
    back_out,
    back_in,
    stat_own,
    stat_mid,
    stat_z,
    stat_c,
    weights_sem,
    down_sem,
    a_send,
    a_recv,
    b_send,
    b_recv,
    s_send,
    s_recv,
    t_send,
    t_recv,
    zs_send,
    zs_recv,
    cs_send,
    cs_recv,
):
    E, C, R, cap, D, F, FC, NF, NC, NN = dims
    Q = PACK // cap
    L = D // Q
    LC = NC // Q
    G = E * cap
    me_e = lax.axis_index("expert")
    me_c = lax.axis_index("cuts")

    def ring(me, step, size):
        return lax.rem(me + step, size)

    def gate_copy(i, n):
        cols = pl.ds(pl.multiple_of(n * FC, FC), FC)
        src, dst = ((gate_hbm, w_gate), (up_hbm, w_up))[i]
        return pltpu.make_async_copy(src.at[0, :, cols], dst.at[:, cols], weights_sem.at[i, n])

    def down_copy(n):
        cols = pl.ds(pl.multiple_of(n * NC, NC), NC)
        return pltpu.make_async_copy(down_hbm.at[0, :, cols], w_down.at[:, cols], down_sem.at[n])

    for n in range(NF):
        gate_copy(0, n).start()
        gate_copy(1, n).start()
    for n in range(NN):
        down_copy(n).start()

    barrier = pltpu.get_barrier_semaphore()
    for d in range(1, E):
        pl.semaphore_signal(
            barrier, inc=1, device_id={"expert": ring(me_e, d, E)}, device_id_type=MESH
        )
    for d in range(1, C):
        pl.semaphore_signal(
            barrier, inc=1, device_id={"cuts": ring(me_c, d, C)}, device_id_type=MESH
        )

    ids = ids_ref[...]
    id0, id1 = ids[:, 0:1], ids[:, 1:2]
    row_i = lax.broadcasted_iota(jnp.int32, (R, R), 0)
    col_i = lax.broadcasted_iota(jnp.int32, (R, R), 1)
    id0_row = jnp.sum(jnp.where(row_i == col_i, id0, 0), axis=0, keepdims=True)
    id1_row = jnp.sum(jnp.where(row_i == col_i, id1, 0), axis=0, keepdims=True)
    slot = lax.broadcasted_iota(jnp.int32, (G, R), 0)
    slot_e, slot_j = slot // cap, slot % cap
    named = (id0_row == slot_e) | (id1_row == slot_e)
    before = (row_i < col_i).astype(jnp.float32)
    place = jnp.dot(named.astype(jnp.float32), before, preferred_element_type=jnp.float32)
    chooser = (named & (place == slot_j.astype(jnp.float32))).astype(jnp.bfloat16)
    tokens = tokens_ref[...]
    picked = jnp.dot(chooser, tokens, preferred_element_type=jnp.float32)
    for e in range(E):
        outbox[e] = fold(picked[e * cap : (e + 1) * cap], Q).astype(jnp.bfloat16)
    inbox[me_c, me_e] = outbox[me_e]

    pl.semaphore_wait(barrier, E - 1 + C - 1)

    def to_expert(d):
        peer = ring(me_e, d, E)
        return remote(
            outbox.at[peer], inbox.at[me_c, me_e], a_send.at[d - 1], a_recv.at[d - 1], "expert", peer
        )

    def from_expert(d):
        src = ring(me_e, E - d, E)
        return remote(
            outbox.at[me_e], inbox.at[me_c, src], a_send.at[d - 1], a_recv.at[d - 1], "expert", src
        )

    def to_cut(p, s):
        src = ring(me_e, E - p, E)
        peer = ring(me_c, s, C)
        return remote(
            inbox.at[me_c, src], inbox.at[me_c, src], b_send.at[p, s - 1], b_recv.at[p, s - 1], "cuts", peer
        )

    def from_cut(p, s):
        src = ring(me_e, E - p, E)
        peer = ring(me_c, C - s, C)
        return remote(
            inbox.at[me_c, src], inbox.at[peer, src], b_send.at[p, s - 1], b_recv.at[p, s - 1], "cuts", peer
        )

    for d in range(1, E):
        to_expert(d).start()
    for s in range(1, C):
        to_cut(0, s).start()

    wide = tokens.astype(jnp.float32)
    exps = []
    for e in range(E):
        weight = router_ref[e : e + 1, :].astype(jnp.float32)
        exps.append(jnp.exp(jnp.sum(wide * weight, axis=1, keepdims=True)))
    total = functools.reduce(jnp.add, exps)
    log_total = jnp.log(total)
    probs = [x / total for x in exps]
    member = [((id0 == e) | (id1 == e)).astype(jnp.float32) for e in range(E)]
    chosen = functools.reduce(jnp.add, [m * p for m, p in zip(member, probs)])
    lane = lax.broadcasted_iota(jnp.int32, (R, 128), 1)
    first = jnp.where(lane == E, log_total * log_total, 0.0)
    second = jnp.zeros((R, 128), jnp.float32)
    for e in range(E):
        first = jnp.where(lane == e, probs[e], first)
        second = jnp.where(lane == e, member[e], second)
    stat_own[0] = first
    stat_own[1] = second

    spot = lax.broadcasted_iota(jnp.int32, (R, G), 1)
    spot_e, spot_j = spot // cap, spot % cap
    named_t = ((id0 == spot_e) | (id1 == spot_e))
    after = (col_i < row_i).astype(jnp.float32)
    place_t = jnp.dot(after, named_t.astype(jnp.float32), preferred_element_type=jnp.float32)
    mix = jnp.zeros((R, G), jnp.float32)
    for e in range(E):
        mix = jnp.where(spot_e == e, probs[e] / chosen, mix)
    mix = jnp.where(named_t & (place_t == spot_j.astype(jnp.float32)), mix, 0.0)

    def stat_to_expert(d):
        peer = ring(me_e, d, E)
        return remote(stat_own, stat_z.at[d - 1], zs_send.at[d - 1], zs_recv.at[d - 1], "expert", peer)

    def stat_to_cut(s):
        peer = ring(me_c, s, C)
        return remote(stat_mid, stat_c.at[s - 1], cs_send.at[s - 1], cs_recv.at[s - 1], "cuts", peer)

    for d in range(1, E):
        stat_to_expert(d).start()

    for d in range(1, E):
        from_expert(d).wait_recv()
        for s in range(1, C):
            to_cut(d, s).start()

    def unpack(s):
        owner = ring(me_c, C - s, C)
        arrived = inbox[owner].astype(jnp.float32)
        for q in range(Q):
            rows = jnp.concatenate(
                [arrived[e, q * cap : (q + 1) * cap, :] for e in range(E)], axis=0
            )
            block[pl.ds(pl.multiple_of(owner * G, G), G), q * L : (q + 1) * L] = rows.astype(
                jnp.bfloat16
            )

    unpack(0)
    for d in range(1, E):
        stat_to_expert(d).wait_recv()
    stat = jnp.zeros(stat_own.shape, jnp.float32)
    for e in range(E):
        term = jnp.where(me_e == e, stat_own[...], 0.0)
        for d in range(1, E):
            term = term + jnp.where(ring(me_e, E - d, E) == e, stat_z[d - 1], 0.0)
        stat = stat + term
    stat_mid[...] = stat
    for s in range(1, C):
        stat_to_cut(s).start()

    @pl.loop(1, C)
    def _(s):
        for p in range(E):
            from_cut(p, s).wait_recv()
        unpack(s)

    @pl.loop(0, NF)
    def _(n):
        cols = pl.ds(pl.multiple_of(n * FC, FC), FC)
        gate_copy(0, n).wait()
        gate = jnp.dot(block[...], w_gate[:, cols], preferred_element_type=jnp.float32)
        gate_copy(1, n).wait()
        upper = jnp.dot(block[...], w_up[:, cols], preferred_element_type=jnp.float32)
        hidden[:, cols] = (gate / (1.0 + jnp.exp(-gate)) * upper).astype(jnp.bfloat16)

    def to_sum(n, s):
        peer = ring(me_c, s, C)
        rows = pl.ds(pl.multiple_of(peer * G, G), G)
        return remote(
            partial.at[n, rows], sums_in.at[n, s - 1], s_send.at[n, s - 1], s_recv.at[n, s - 1], "cuts", peer
        )

    def to_owner(n, d):
        peer = ring(me_e, d, E)
        return remote(
            back_out.at[n, peer], back_in.at[n, me_e], t_send.at[n, d - 1], t_recv.at[n, d - 1], "expert", peer
        )

    def from_owner(n, d):
        src = ring(me_e, E - d, E)
        return remote(
            back_out.at[n, me_e], back_in.at[n, src], t_send.at[n, d - 1], t_recv.at[n, d - 1], "expert", src
        )

    def stage_down(n):
        cols = pl.ds(pl.multiple_of(n * NC, NC), NC)
        down_copy(n).wait()
        partial[n] = jnp.dot(
            hidden[...], w_down[:, cols], preferred_element_type=jnp.float32
        ).astype(jnp.bfloat16)
        for s in range(1, C):
            to_sum(n, s).start()

    def stage_sum(n):
        rows = pl.ds(pl.multiple_of(me_c * G, G), G)
        acc = partial[n, rows].astype(jnp.float32)
        for s in range(1, C):
            to_sum(n, s).wait_recv()
            acc = acc + sums_in[n, s - 1].astype(jnp.float32)
        for e in range(E):
            back_out[n, e] = fold(acc[e * cap : (e + 1) * cap], Q).astype(jnp.bfloat16)
        for d in range(1, E):
            to_owner(n, d).start()
        back_in[n, me_e] = back_out[n, me_e]

    def stage_mix(n):
        for d in range(1, E):
            from_owner(n, d).wait_recv()
        got = back_in[n].astype(jnp.float32)
        wide = jnp.concatenate(
            [
                jnp.concatenate([got[e, q * cap : (q + 1) * cap, :] for e in range(E)], axis=0)
                for q in range(Q)
            ],
            axis=1,
        )
        out = jnp.dot(
            mix, wide, preferred_element_type=jnp.float32, precision=lax.Precision.HIGHEST
        )
        mixed_ref[:, n * NC : (n + 1) * NC] = out.astype(jnp.bfloat16)

    for n in range(NN + 2):
        if n < NN:
            stage_down(n)
        if 1 <= n <= NN:
            stage_sum(n - 1)
        if n >= 2:
            stage_mix(n - 2)

    for s in range(1, C):
        stat_to_cut(s).wait_recv()
    stat = jnp.zeros(stat_own.shape, jnp.float32)
    for c in range(C):
        term = jnp.where(me_c == c, stat_mid[...], 0.0)
        for s in range(1, C):
            term = term + jnp.where(ring(me_c, C - s, C) == c, stat_c[s - 1], 0.0)
        stat = stat + term
    rows = float(R * E * C)
    one = jnp.sum(stat[0], axis=0, keepdims=True) / rows
    two = jnp.sum(stat[1], axis=0, keepdims=True) / (rows * 2.0)
    lane = lax.broadcasted_iota(jnp.int32, (1, 128), 1)
    stats_ref[0] = jnp.sum(jnp.where(lane == E, one, 0.0))
    stats_ref[1] = E * jnp.sum(jnp.where(lane < E, one * two, 0.0))

    for d in range(1, E):
        to_expert(d).wait_send()
        stat_to_expert(d).wait_send()
        for n in range(NN):
            to_owner(n, d).wait_send()
    for s in range(1, C):
        stat_to_cut(s).wait_send()
        for p in range(E):
            to_cut(p, s).wait_send()
        for n in range(NN):
            to_sum(n, s).wait_send()


def shards(tokens, router_weight, gate_weight, up_weight, down_weight, expert_ids):
    R, D = tokens.shape
    E = lax.axis_size("expert")
    C = lax.axis_size("cuts")
    F = gate_weight.shape[2]
    cap = R // 2
    Q = PACK // cap
    FC = min(512, F)
    NF = F // FC
    NC = min(1024, D)
    NN = D // NC
    G = E * cap
    rows = C * G
    dims = (E, C, R, cap, D, F, FC, NF, NC, NN)
    bf16, f32 = jnp.bfloat16, jnp.float32
    vmem = pl.BlockSpec(memory_space=pltpu.VMEM)
    hbm = pl.BlockSpec(memory_space=pl.ANY)
    dma = pltpu.SemaphoreType.DMA
    return pl.pallas_call(
        functools.partial(kernel, dims),
        out_shape=(
            jax.ShapeDtypeStruct((R, D), bf16),
            jax.ShapeDtypeStruct((2,), f32),
        ),
        in_specs=[vmem, vmem, vmem, hbm, hbm, hbm],
        out_specs=(vmem, pl.BlockSpec(memory_space=pltpu.SMEM)),
        scratch_shapes=[
            pltpu.VMEM((D, F), bf16),
            pltpu.VMEM((D, F), bf16),
            pltpu.VMEM((F, D), bf16),
            pltpu.VMEM((E, PACK, D // Q), bf16),
            pltpu.VMEM((C, E, PACK, D // Q), bf16),
            pltpu.VMEM((rows, D), bf16),
            pltpu.VMEM((rows, F), bf16),
            pltpu.VMEM((NN, rows, NC), bf16),
            pltpu.VMEM((NN, C - 1, G, NC), bf16),
            pltpu.VMEM((NN, E, PACK, NC // Q), bf16),
            pltpu.VMEM((NN, E, PACK, NC // Q), bf16),
            pltpu.VMEM((2, R, 128), f32),
            pltpu.VMEM((2, R, 128), f32),
            pltpu.VMEM((E - 1, 2, R, 128), f32),
            pltpu.VMEM((C - 1, 2, R, 128), f32),
            dma((2, NF)),
            dma((NN,)),
            dma((E - 1,)),
            dma((E - 1,)),
            dma((E, C - 1)),
            dma((E, C - 1)),
            dma((NN, C - 1)),
            dma((NN, C - 1)),
            dma((NN, E - 1)),
            dma((NN, E - 1)),
            dma((E - 1,)),
            dma((E - 1,)),
            dma((C - 1,)),
            dma((C - 1,)),
        ],
        compiler_params=pltpu.CompilerParams(
            collective_id=0, has_side_effects=True, vmem_limit_bytes=60 * 1024 * 1024
        ),
        cost_estimate=pl.CostEstimate(
            flops=6 * rows * D * F, bytes_accessed=6 * D * F, transcendentals=rows * F
        ),
    )(tokens, router_weight.T, expert_ids, gate_weight, up_weight, down_weight)


def solution(mesh):
    placed = (
        P(("groups", "expert", "cuts"), None),
        P(),
        P("expert", None, "cuts"),
        P("expert", None, "cuts"),
        P("expert", "cuts", None),
        P(("groups", "expert", "cuts"), None),
    )
    return jax.shard_map(
        shards,
        mesh=mesh,
        in_specs=placed,
        out_specs=(P(("groups", "expert", "cuts"), None), P("groups")),
        check_vma=False,
    )
```

```python
import functools

import jax
import jax.numpy as jnp
from jax import lax
from jax.experimental import pallas as pl
from jax.experimental.pallas import tpu as pltpu
from jax.sharding import PartitionSpec as P

MESH = pl.DeviceIdType.MESH
PACK = 16
LAG = 4


def remote(src, dst, send, recv, axis, peer):
    return pltpu.make_async_remote_copy(
        src_ref=src,
        dst_ref=dst,
        send_sem=send,
        recv_sem=recv,
        device_id={axis: peer},
        device_id_type=MESH,
    )


def fold(rows, parts):
    lanes = rows.shape[1] // parts
    return jnp.concatenate([rows[:, q * lanes : (q + 1) * lanes] for q in range(parts)], axis=0)


def hand_on(rows_ref, stats_ref, rows_out, stats_out):
    rows_out[...] = rows_ref[...]
    stats_out[0] = stats_ref[0]
    stats_out[1] = stats_ref[1]


def kernel(
    dims,
    tokens_ref,
    router_ref,
    ids_ref,
    gate_hbm,
    up_hbm,
    down_hbm,
    mixed_ref,
    stats_ref,
    w_gate,
    w_up,
    w_down,
    outbox,
    inbox,
    block,
    hidden,
    partial,
    sums_in,
    back_out,
    back_in,
    stat_own,
    stat_mid,
    stat_z,
    stat_c,
    weights_sem,
    down_sem,
    a_send,
    a_recv,
    b_send,
    b_recv,
    s_send,
    s_recv,
    t_send,
    t_recv,
    zs_send,
    zs_recv,
    cs_send,
    cs_recv,
):
    E, C, R, cap, D, F, FC, NF, NC, NN = dims
    Q = PACK // cap
    L = D // Q
    LC = NC // Q
    G = E * cap
    me_e = lax.axis_index("expert")
    me_c = lax.axis_index("cuts")

    def ring(me, step, size):
        return lax.rem(me + step, size)

    def gate_copy(i, n):
        cols = pl.ds(pl.multiple_of(n * FC, FC), FC)
        src, dst = ((gate_hbm, w_gate), (up_hbm, w_up))[i]
        return pltpu.make_async_copy(src.at[0, :, cols], dst.at[:, cols], weights_sem.at[i, n])

    def down_copy(n):
        cols = pl.ds(pl.multiple_of(n * NC, NC), NC)
        return pltpu.make_async_copy(down_hbm.at[0, :, cols], w_down.at[:, cols], down_sem.at[n])

    for n in range(NF):
        gate_copy(0, n).start()
        gate_copy(1, n).start()
    for n in range(NN):
        down_copy(n).start()

    barrier = pltpu.get_barrier_semaphore()
    for d in range(1, E):
        pl.semaphore_signal(
            barrier, inc=1, device_id={"expert": ring(me_e, d, E)}, device_id_type=MESH
        )
    for d in range(1, C):
        pl.semaphore_signal(
            barrier, inc=1, device_id={"cuts": ring(me_c, d, C)}, device_id_type=MESH
        )

    ids = ids_ref[...]
    id0_row, id1_row = ids[0:1, :], ids[1:2, :]
    row_i = lax.broadcasted_iota(jnp.int32, (R, R), 0)
    col_i = lax.broadcasted_iota(jnp.int32, (R, R), 1)
    id0 = jnp.sum(jnp.where(row_i == col_i, id0_row, 0), axis=1, keepdims=True)
    id1 = jnp.sum(jnp.where(row_i == col_i, id1_row, 0), axis=1, keepdims=True)
    slot = lax.broadcasted_iota(jnp.int32, (G, R), 0)
    slot_e, slot_j = slot // cap, slot % cap
    named = (id0_row == slot_e) | (id1_row == slot_e)
    before = (row_i < col_i).astype(jnp.float32)
    place = jnp.dot(named.astype(jnp.float32), before, preferred_element_type=jnp.float32)
    chooser = (named & (place == slot_j.astype(jnp.float32))).astype(jnp.bfloat16)
    tokens = tokens_ref[...]
    picked = jnp.dot(chooser, tokens, preferred_element_type=jnp.float32)
    for e in range(E):
        outbox[e] = fold(picked[e * cap : (e + 1) * cap], Q).astype(jnp.bfloat16)
    inbox[me_c, me_e] = outbox[me_e]

    pl.semaphore_wait(barrier, E - 1 + C - 1)

    def to_expert(d):
        peer = ring(me_e, d, E)
        return remote(
            outbox.at[peer], inbox.at[me_c, me_e], a_send.at[d - 1], a_recv.at[d - 1], "expert", peer
        )

    def from_expert(d):
        src = ring(me_e, E - d, E)
        return remote(
            outbox.at[me_e], inbox.at[me_c, src], a_send.at[d - 1], a_recv.at[d - 1], "expert", src
        )

    def to_cut(p, s):
        src = ring(me_e, E - p, E)
        peer = ring(me_c, s, C)
        return remote(
            inbox.at[me_c, src], inbox.at[me_c, src], b_send.at[p, s - 1], b_recv.at[p, s - 1], "cuts", peer
        )

    def from_cut(p, s):
        src = ring(me_e, E - p, E)
        peer = ring(me_c, C - s, C)
        return remote(
            inbox.at[me_c, src], inbox.at[peer, src], b_send.at[p, s - 1], b_recv.at[p, s - 1], "cuts", peer
        )

    for d in range(1, E):
        to_expert(d).start()
    for s in range(1, C):
        to_cut(0, s).start()

    for d in range(1, E):
        from_expert(d).wait_recv()
        for s in range(1, C):
            to_cut(d, s).start()

    wide = tokens.astype(jnp.float32)
    exps = []
    for e in range(E):
        weight = router_ref[e : e + 1, :].astype(jnp.float32)
        exps.append(jnp.exp(jnp.sum(wide * weight, axis=1, keepdims=True)))
    total = functools.reduce(jnp.add, exps)
    log_total = jnp.log(total)
    probs = [x / total for x in exps]
    member = [((id0 == e) | (id1 == e)).astype(jnp.float32) for e in range(E)]
    chosen = functools.reduce(jnp.add, [m * p for m, p in zip(member, probs)])
    lane = lax.broadcasted_iota(jnp.int32, (R, 128), 1)
    first = jnp.where(lane == E, log_total * log_total, 0.0)
    second = jnp.zeros((R, 128), jnp.float32)
    for e in range(E):
        first = jnp.where(lane == e, probs[e], first)
        second = jnp.where(lane == e, member[e], second)
    stat_own[0] = first
    stat_own[1] = second

    spot = lax.broadcasted_iota(jnp.int32, (R, G), 1)
    spot_e, spot_j = spot // cap, spot % cap
    named_t = ((id0 == spot_e) | (id1 == spot_e))
    after = (col_i < row_i).astype(jnp.float32)
    place_t = jnp.dot(after, named_t.astype(jnp.float32), preferred_element_type=jnp.float32)
    mix = jnp.zeros((R, G), jnp.float32)
    for e in range(E):
        mix = jnp.where(spot_e == e, probs[e] / chosen, mix)
    mix = jnp.where(named_t & (place_t == spot_j.astype(jnp.float32)), mix, 0.0)

    def stat_to_expert(d):
        peer = ring(me_e, d, E)
        return remote(stat_own, stat_z.at[d - 1], zs_send.at[d - 1], zs_recv.at[d - 1], "expert", peer)

    def stat_to_cut(s):
        peer = ring(me_c, s, C)
        return remote(stat_mid, stat_c.at[s - 1], cs_send.at[s - 1], cs_recv.at[s - 1], "cuts", peer)

    for d in range(1, E):
        stat_to_expert(d).start()

    def unpack(s):
        owner = ring(me_c, C - s, C)
        arrived = inbox[owner].astype(jnp.float32)
        for q in range(Q):
            rows = jnp.concatenate(
                [arrived[e, q * cap : (q + 1) * cap, :] for e in range(E)], axis=0
            )
            block[pl.ds(pl.multiple_of(owner * G, G), G), q * L : (q + 1) * L] = rows.astype(
                jnp.bfloat16
            )

    unpack(0)
    @pl.loop(1, C)
    def _(s):
        for p in range(E):
            from_cut(p, s).wait_recv()
        unpack(s)

    @pl.loop(0, NF)
    def _(n):
        cols = pl.ds(pl.multiple_of(n * FC, FC), FC)
        gate_copy(0, n).wait()
        gate = jnp.dot(block[...], w_gate[:, cols], preferred_element_type=jnp.float32)
        gate_copy(1, n).wait()
        upper = jnp.dot(block[...], w_up[:, cols], preferred_element_type=jnp.float32)
        hidden[:, cols] = (gate / (1.0 + jnp.exp(-gate)) * upper).astype(jnp.bfloat16)

    for d in range(1, E):
        stat_to_expert(d).wait_recv()
    stat = jnp.zeros(stat_own.shape, jnp.float32)
    for e in range(E):
        term = jnp.where(me_e == e, stat_own[...], 0.0)
        for d in range(1, E):
            term = term + jnp.where(ring(me_e, E - d, E) == e, stat_z[d - 1], 0.0)
        stat = stat + term
    stat_mid[...] = stat
    for s in range(1, C):
        stat_to_cut(s).start()

    def to_sum(n, s):
        peer = ring(me_c, s, C)
        rows = pl.ds(pl.multiple_of(peer * G, G), G)
        return remote(
            partial.at[n, rows], sums_in.at[n, s - 1], s_send.at[n, s - 1], s_recv.at[n, s - 1], "cuts", peer
        )

    def to_owner(n, d):
        peer = ring(me_e, d, E)
        return remote(
            back_out.at[n, peer], back_in.at[n, me_e], t_send.at[n, d - 1], t_recv.at[n, d - 1], "expert", peer
        )

    def from_owner(n, d):
        src = ring(me_e, E - d, E)
        return remote(
            back_out.at[n, me_e], back_in.at[n, src], t_send.at[n, d - 1], t_recv.at[n, d - 1], "expert", src
        )

    def stage_down(n):
        cols = pl.ds(pl.multiple_of(n * NC, NC), NC)
        down_copy(n).wait()
        partial[n] = jnp.dot(
            hidden[...], w_down[:, cols], preferred_element_type=jnp.float32
        ).astype(jnp.bfloat16)
        for s in range(1, C):
            to_sum(n, s).start()

    def stage_sum(n):
        rows = pl.ds(pl.multiple_of(me_c * G, G), G)
        acc = partial[n, rows].astype(jnp.float32)
        for s in range(1, C):
            to_sum(n, s).wait_recv()
            acc = acc + sums_in[n, s - 1].astype(jnp.float32)
        for e in range(E):
            back_out[n, e] = fold(acc[e * cap : (e + 1) * cap], Q).astype(jnp.bfloat16)
        for d in range(1, E):
            to_owner(n, d).start()
        back_in[n, me_e] = back_out[n, me_e]

    def stage_mix(n):
        for d in range(1, E):
            from_owner(n, d).wait_recv()
        got = back_in[n].astype(jnp.float32)
        wide = jnp.concatenate(
            [
                jnp.concatenate([got[e, q * cap : (q + 1) * cap, :] for e in range(E)], axis=0)
                for q in range(Q)
            ],
            axis=1,
        )
        out = jnp.dot(
            mix, wide, preferred_element_type=jnp.float32, precision=lax.Precision.HIGHEST
        )
        mixed_ref[:, n * NC : (n + 1) * NC] = out.astype(jnp.bfloat16)

    for n in range(NN + 2 * LAG):
        if n < NN:
            stage_down(n)
        if LAG <= n < NN + LAG:
            stage_sum(n - LAG)
        if n >= 2 * LAG:
            stage_mix(n - 2 * LAG)

    for s in range(1, C):
        stat_to_cut(s).wait_recv()
    stat = jnp.zeros(stat_own.shape, jnp.float32)
    for c in range(C):
        term = jnp.where(me_c == c, stat_mid[...], 0.0)
        for s in range(1, C):
            term = term + jnp.where(ring(me_c, C - s, C) == c, stat_c[s - 1], 0.0)
        stat = stat + term
    rows = float(R * E * C)
    one = jnp.sum(stat[0], axis=0, keepdims=True) / rows
    two = jnp.sum(stat[1], axis=0, keepdims=True) / (rows * 2.0)
    lane = lax.broadcasted_iota(jnp.int32, (1, 128), 1)
    stats_ref[0] = jnp.sum(jnp.where(lane == E, one, 0.0))
    stats_ref[1] = E * jnp.sum(jnp.where(lane < E, one * two, 0.0))

    for d in range(1, E):
        to_expert(d).wait_send()
        stat_to_expert(d).wait_send()
        for n in range(NN):
            to_owner(n, d).wait_send()
    for s in range(1, C):
        stat_to_cut(s).wait_send()
        for p in range(E):
            to_cut(p, s).wait_send()
        for n in range(NN):
            to_sum(n, s).wait_send()


def shards(tokens, router_weight, gate_weight, up_weight, down_weight, expert_ids):
    R, D = tokens.shape
    E = lax.axis_size("expert")
    C = lax.axis_size("cuts")
    F = gate_weight.shape[2]
    cap = R // 2
    Q = PACK // cap
    FC = min(512, F)
    NF = F // FC
    NC = min(1024, D)
    NN = D // NC
    G = E * cap
    rows = C * G
    dims = (E, C, R, cap, D, F, FC, NF, NC, NN)
    bf16, f32 = jnp.bfloat16, jnp.float32
    vmem = pl.BlockSpec(memory_space=pltpu.VMEM)
    hbm = pl.BlockSpec(memory_space=pl.ANY)
    dma = pltpu.SemaphoreType.DMA
    rows_out, stats = pl.pallas_call(
        functools.partial(kernel, dims),
        out_shape=(
            jax.ShapeDtypeStruct((R, D), bf16),
            jax.ShapeDtypeStruct((2,), f32),
        ),
        in_specs=[vmem, vmem, vmem, hbm, hbm, hbm],
        out_specs=(vmem, pl.BlockSpec(memory_space=pltpu.SMEM)),
        scratch_shapes=[
            pltpu.VMEM((D, F), bf16),
            pltpu.VMEM((D, F), bf16),
            pltpu.VMEM((F, D), bf16),
            pltpu.VMEM((E, PACK, D // Q), bf16),
            pltpu.VMEM((C, E, PACK, D // Q), bf16),
            pltpu.VMEM((rows, D), bf16),
            pltpu.VMEM((rows, F), bf16),
            pltpu.VMEM((NN, rows, NC), bf16),
            pltpu.VMEM((NN, C - 1, G, NC), bf16),
            pltpu.VMEM((NN, E, PACK, NC // Q), bf16),
            pltpu.VMEM((NN, E, PACK, NC // Q), bf16),
            pltpu.VMEM((2, R, 128), f32),
            pltpu.VMEM((2, R, 128), f32),
            pltpu.VMEM((E - 1, 2, R, 128), f32),
            pltpu.VMEM((C - 1, 2, R, 128), f32),
            dma((2, NF)),
            dma((NN,)),
            dma((E - 1,)),
            dma((E - 1,)),
            dma((E, C - 1)),
            dma((E, C - 1)),
            dma((NN, C - 1)),
            dma((NN, C - 1)),
            dma((NN, E - 1)),
            dma((NN, E - 1)),
            dma((E - 1,)),
            dma((E - 1,)),
            dma((C - 1,)),
            dma((C - 1,)),
        ],
        compiler_params=pltpu.CompilerParams(
            collective_id=0, has_side_effects=True, vmem_limit_bytes=60 * 1024 * 1024
        ),
        cost_estimate=pl.CostEstimate(
            flops=6 * rows * D * F, bytes_accessed=6 * D * F, transcendentals=rows * F
        ),
    )(tokens, router_weight.T, expert_ids.T, gate_weight, up_weight, down_weight)
    smem = pl.BlockSpec(memory_space=pltpu.SMEM)
    return pl.pallas_call(
        hand_on,
        out_shape=(jax.ShapeDtypeStruct((R, D), bf16), jax.ShapeDtypeStruct((2,), f32)),
        in_specs=[vmem, smem],
        out_specs=(vmem, smem),
    )(rows_out, stats)


def solution(mesh):
    placed = (
        P(("groups", "expert", "cuts"), None),
        P(),
        P("expert", None, "cuts"),
        P("expert", None, "cuts"),
        P("expert", "cuts", None),
        P(("groups", "expert", "cuts"), None),
    )
    return jax.shard_map(
        shards,
        mesh=mesh,
        in_specs=placed,
        out_specs=(P(("groups", "expert", "cuts"), None), P("groups")),
        check_vma=False,
    )
```

```python
import functools

import jax
import jax.numpy as jnp
from jax import lax
from jax.experimental import pallas as pl
from jax.experimental.pallas import tpu as pltpu
from jax.sharding import PartitionSpec as P

MESH = pl.DeviceIdType.MESH
PACK = 16
LAG = 4


def remote(src, dst, send, recv, axis, peer):
    return pltpu.make_async_remote_copy(
        src_ref=src,
        dst_ref=dst,
        send_sem=send,
        recv_sem=recv,
        device_id={axis: peer},
        device_id_type=MESH,
    )


def fold(rows, parts):
    lanes = rows.shape[1] // parts
    return jnp.concatenate([rows[:, q * lanes : (q + 1) * lanes] for q in range(parts)], axis=0)


def hand_on(rows_ref, stats_ref, rows_out, stats_out):
    rows_out[...] = rows_ref[...]
    stats_out[0] = stats_ref[0]
    stats_out[1] = stats_ref[1]


def kernel(
    dims,
    tokens_ref,
    router_ref,
    ids_ref,
    gate_hbm,
    up_hbm,
    down_hbm,
    mixed_ref,
    stats_ref,
    w_gate,
    w_up,
    w_down,
    outbox,
    inbox,
    block,
    hidden,
    partial,
    sums_in,
    back_out,
    back_in,
    stat_own,
    stat_mid,
    stat_z,
    stat_c,
    weights_sem,
    down_sem,
    a_send,
    a_recv,
    b_send,
    b_recv,
    s_send,
    s_recv,
    t_send,
    t_recv,
    zs_send,
    zs_recv,
    cs_send,
    cs_recv,
):
    E, C, R, cap, D, F, FC, NF, NC, NN = dims
    Q = PACK // cap
    L = D // Q
    LC = NC // Q
    G = E * cap
    me_e = lax.axis_index("expert")
    me_c = lax.axis_index("cuts")

    def ring(me, step, size):
        return lax.rem(me + step, size)

    def gate_copy(i, n):
        cols = pl.ds(pl.multiple_of(n * FC, FC), FC)
        src, dst = ((gate_hbm, w_gate), (up_hbm, w_up))[i]
        return pltpu.make_async_copy(src.at[0, :, cols], dst.at[:, cols], weights_sem.at[i, n])

    def down_copy(n):
        cols = pl.ds(pl.multiple_of(n * NC, NC), NC)
        return pltpu.make_async_copy(down_hbm.at[0, :, cols], w_down.at[:, cols], down_sem.at[n])

    for n in range(NF):
        gate_copy(0, n).start()
        gate_copy(1, n).start()
    for n in range(NN):
        down_copy(n).start()

    barrier = pltpu.get_barrier_semaphore()
    for d in range(1, E):
        pl.semaphore_signal(
            barrier, inc=1, device_id={"expert": ring(me_e, d, E)}, device_id_type=MESH
        )
    for d in range(1, C):
        pl.semaphore_signal(
            barrier, inc=1, device_id={"cuts": ring(me_c, d, C)}, device_id_type=MESH
        )

    ids = ids_ref[...]
    id0_row, id1_row = ids[0:1, :], ids[1:2, :]
    row_i = lax.broadcasted_iota(jnp.int32, (R, R), 0)
    col_i = lax.broadcasted_iota(jnp.int32, (R, R), 1)
    id0 = jnp.sum(jnp.where(row_i == col_i, id0_row, 0), axis=1, keepdims=True)
    id1 = jnp.sum(jnp.where(row_i == col_i, id1_row, 0), axis=1, keepdims=True)
    slot = lax.broadcasted_iota(jnp.int32, (G, R), 0)
    slot_e, slot_j = slot // cap, slot % cap
    named = (id0_row == slot_e) | (id1_row == slot_e)
    before = (row_i < col_i).astype(jnp.float32)
    place = jnp.dot(named.astype(jnp.float32), before, preferred_element_type=jnp.float32)
    chooser = (named & (place == slot_j.astype(jnp.float32))).astype(jnp.bfloat16)
    tokens = tokens_ref[...]
    picked = jnp.dot(chooser, tokens, preferred_element_type=jnp.float32)
    for e in range(E):
        outbox[e] = fold(picked[e * cap : (e + 1) * cap], Q).astype(jnp.bfloat16)
    inbox[me_c, me_e] = outbox[me_e]

    pl.semaphore_wait(barrier, E - 1 + C - 1)

    def to_expert(d):
        peer = ring(me_e, d, E)
        return remote(
            outbox.at[peer], inbox.at[me_c, me_e], a_send.at[d - 1], a_recv.at[d - 1], "expert", peer
        )

    def from_expert(d):
        src = ring(me_e, E - d, E)
        return remote(
            outbox.at[me_e], inbox.at[me_c, src], a_send.at[d - 1], a_recv.at[d - 1], "expert", src
        )

    def to_cut(p, s):
        src = ring(me_e, E - p, E)
        peer = ring(me_c, s, C)
        return remote(
            inbox.at[me_c, src], inbox.at[me_c, src], b_send.at[p, s - 1], b_recv.at[p, s - 1], "cuts", peer
        )

    def from_cut(p, s):
        src = ring(me_e, E - p, E)
        peer = ring(me_c, C - s, C)
        return remote(
            inbox.at[me_c, src], inbox.at[peer, src], b_send.at[p, s - 1], b_recv.at[p, s - 1], "cuts", peer
        )

    for d in range(1, E):
        to_expert(d).start()
    for s in range(1, C):
        to_cut(0, s).start()

    for d in range(1, E):
        from_expert(d).wait_recv()
        for s in range(1, C):
            to_cut(d, s).start()

    wide = tokens.astype(jnp.float32)
    exps = []
    for e in range(E):
        weight = router_ref[e : e + 1, :].astype(jnp.float32)
        exps.append(jnp.exp(jnp.sum(wide * weight, axis=1, keepdims=True)))
    total = functools.reduce(jnp.add, exps)
    log_total = jnp.log(total)
    probs = [x / total for x in exps]
    member = [((id0 == e) | (id1 == e)).astype(jnp.float32) for e in range(E)]
    chosen = functools.reduce(jnp.add, [m * p for m, p in zip(member, probs)])
    lane = lax.broadcasted_iota(jnp.int32, (R, 128), 1)
    first = jnp.where(lane == E, log_total * log_total, 0.0)
    second = jnp.zeros((R, 128), jnp.float32)
    for e in range(E):
        first = jnp.where(lane == e, probs[e], first)
        second = jnp.where(lane == e, member[e], second)
    stat_own[0] = first
    stat_own[1] = second

    spot = lax.broadcasted_iota(jnp.int32, (R, G), 1)
    spot_e, spot_j = spot // cap, spot % cap
    named_t = ((id0 == spot_e) | (id1 == spot_e))
    after = (col_i < row_i).astype(jnp.float32)
    place_t = jnp.dot(after, named_t.astype(jnp.float32), preferred_element_type=jnp.float32)
    mix = jnp.zeros((R, G), jnp.float32)
    for e in range(E):
        mix = jnp.where(spot_e == e, probs[e] / chosen, mix)
    mix = jnp.where(named_t & (place_t == spot_j.astype(jnp.float32)), mix, 0.0)

    def stat_to_expert(d):
        peer = ring(me_e, d, E)
        return remote(stat_own, stat_z.at[d - 1], zs_send.at[d - 1], zs_recv.at[d - 1], "expert", peer)

    def stat_to_cut(s):
        peer = ring(me_c, s, C)
        return remote(stat_mid, stat_c.at[s - 1], cs_send.at[s - 1], cs_recv.at[s - 1], "cuts", peer)

    for d in range(1, E):
        stat_to_expert(d).start()

    def unpack(s):
        owner = ring(me_c, C - s, C)
        arrived = inbox[owner].astype(jnp.float32)
        for q in range(Q):
            rows = jnp.concatenate(
                [arrived[e, q * cap : (q + 1) * cap, :] for e in range(E)], axis=0
            )
            block[pl.ds(pl.multiple_of(owner * G, G), G), q * L : (q + 1) * L] = rows.astype(
                jnp.bfloat16
            )

    unpack(0)
    @pl.loop(1, C)
    def _(s):
        for p in range(E):
            from_cut(p, s).wait_recv()
        unpack(s)

    @pl.loop(0, NF)
    def _(n):
        cols = pl.ds(pl.multiple_of(n * FC, FC), FC)
        gate_copy(0, n).wait()
        gate = jnp.dot(block[...], w_gate[:, cols], preferred_element_type=jnp.float32)
        gate_copy(1, n).wait()
        upper = jnp.dot(block[...], w_up[:, cols], preferred_element_type=jnp.float32)
        hidden[:, cols] = (gate / (1.0 + jnp.exp(-gate)) * upper).astype(jnp.bfloat16)

    for d in range(1, E):
        stat_to_expert(d).wait_recv()
    stat = jnp.zeros(stat_own.shape, jnp.float32)
    for e in range(E):
        term = jnp.where(me_e == e, stat_own[...], 0.0)
        for d in range(1, E):
            term = term + jnp.where(ring(me_e, E - d, E) == e, stat_z[d - 1], 0.0)
        stat = stat + term
    stat_mid[...] = stat
    for s in range(1, C):
        stat_to_cut(s).start()

    def to_sum(n, s):
        peer = ring(me_c, s, C)
        rows = pl.ds(pl.multiple_of(peer * G, G), G)
        return remote(
            partial.at[n, rows], sums_in.at[n, s - 1], s_send.at[n, s - 1], s_recv.at[n, s - 1], "cuts", peer
        )

    def to_owner(n, d):
        peer = ring(me_e, d, E)
        return remote(
            back_out.at[n, peer], back_in.at[n, me_e], t_send.at[n, d - 1], t_recv.at[n, d - 1], "expert", peer
        )

    def from_owner(n, d):
        src = ring(me_e, E - d, E)
        return remote(
            back_out.at[n, me_e], back_in.at[n, src], t_send.at[n, d - 1], t_recv.at[n, d - 1], "expert", src
        )

    def stage_down(n):
        cols = pl.ds(pl.multiple_of(n * NC, NC), NC)
        down_copy(n).wait()
        partial[n] = jnp.dot(
            hidden[...], w_down[:, cols], preferred_element_type=jnp.float32
        ).astype(jnp.bfloat16)
        for s in range(1, C):
            to_sum(n, s).start()

    def stage_sum(n):
        rows = pl.ds(pl.multiple_of(me_c * G, G), G)
        acc = partial[n, rows].astype(jnp.float32)
        for s in range(1, C):
            to_sum(n, s).wait_recv()
            acc = acc + sums_in[n, s - 1].astype(jnp.float32)
        for e in range(E):
            back_out[n, e] = fold(acc[e * cap : (e + 1) * cap], Q).astype(jnp.bfloat16)
        for d in range(1, E):
            to_owner(n, d).start()
        back_in[n, me_e] = back_out[n, me_e]

    def stage_mix(n):
        for d in range(1, E):
            from_owner(n, d).wait_recv()
        got = back_in[n].astype(jnp.float32)
        wide = jnp.concatenate(
            [
                jnp.concatenate([got[e, q * cap : (q + 1) * cap, :] for e in range(E)], axis=0)
                for q in range(Q)
            ],
            axis=1,
        )
        out = jnp.dot(
            mix, wide, preferred_element_type=jnp.float32, precision=lax.Precision.HIGHEST
        )
        mixed_ref[:, n * NC : (n + 1) * NC] = out.astype(jnp.bfloat16)

    for n in range(NN + 2 * LAG):
        if n < NN:
            stage_down(n)
        if LAG <= n < NN + LAG:
            stage_sum(n - LAG)
        if n >= 2 * LAG:
            stage_mix(n - 2 * LAG)

    for s in range(1, C):
        stat_to_cut(s).wait_recv()
    stat = jnp.zeros(stat_own.shape, jnp.float32)
    for c in range(C):
        term = jnp.where(me_c == c, stat_mid[...], 0.0)
        for s in range(1, C):
            term = term + jnp.where(ring(me_c, C - s, C) == c, stat_c[s - 1], 0.0)
        stat = stat + term
    rows = float(R * E * C)
    one = jnp.sum(stat[0], axis=0, keepdims=True) / rows
    two = jnp.sum(stat[1], axis=0, keepdims=True) / (rows * 2.0)
    lane = lax.broadcasted_iota(jnp.int32, (1, 128), 1)
    stats_ref[0] = jnp.sum(jnp.where(lane == E, one, 0.0))
    stats_ref[1] = E * jnp.sum(jnp.where(lane < E, one * two, 0.0))

    for d in range(1, E):
        to_expert(d).wait_send()
        stat_to_expert(d).wait_send()
        for n in range(NN):
            to_owner(n, d).wait_send()
    for s in range(1, C):
        stat_to_cut(s).wait_send()
        for p in range(E):
            to_cut(p, s).wait_send()
        for n in range(NN):
            to_sum(n, s).wait_send()


def shards(tokens, router_weight, gate_weight, up_weight, down_weight, expert_ids):
    R, D = tokens.shape
    E = lax.axis_size("expert")
    C = lax.axis_size("cuts")
    F = gate_weight.shape[2]
    cap = R // 2
    Q = PACK // cap
    FC = min(1024, F)
    NF = F // FC
    NC = min(1024, D)
    NN = D // NC
    G = E * cap
    rows = C * G
    dims = (E, C, R, cap, D, F, FC, NF, NC, NN)
    bf16, f32 = jnp.bfloat16, jnp.float32
    vmem = pl.BlockSpec(memory_space=pltpu.VMEM)
    hbm = pl.BlockSpec(memory_space=pl.ANY)
    dma = pltpu.SemaphoreType.DMA
    rows_out, stats = pl.pallas_call(
        functools.partial(kernel, dims),
        out_shape=(
            jax.ShapeDtypeStruct((R, D), bf16),
            jax.ShapeDtypeStruct((2,), f32),
        ),
        in_specs=[vmem, vmem, vmem, hbm, hbm, hbm],
        out_specs=(vmem, pl.BlockSpec(memory_space=pltpu.SMEM)),
        scratch_shapes=[
            pltpu.VMEM((D, F), bf16),
            pltpu.VMEM((D, F), bf16),
            pltpu.VMEM((F, D), bf16),
            pltpu.VMEM((E, PACK, D // Q), bf16),
            pltpu.VMEM((C, E, PACK, D // Q), bf16),
            pltpu.VMEM((rows, D), bf16),
            pltpu.VMEM((rows, F), bf16),
            pltpu.VMEM((NN, rows, NC), bf16),
            pltpu.VMEM((NN, C - 1, G, NC), bf16),
            pltpu.VMEM((NN, E, PACK, NC // Q), bf16),
            pltpu.VMEM((NN, E, PACK, NC // Q), bf16),
            pltpu.VMEM((2, R, 128), f32),
            pltpu.VMEM((2, R, 128), f32),
            pltpu.VMEM((E - 1, 2, R, 128), f32),
            pltpu.VMEM((C - 1, 2, R, 128), f32),
            dma((2, NF)),
            dma((NN,)),
            dma((E - 1,)),
            dma((E - 1,)),
            dma((E, C - 1)),
            dma((E, C - 1)),
            dma((NN, C - 1)),
            dma((NN, C - 1)),
            dma((NN, E - 1)),
            dma((NN, E - 1)),
            dma((E - 1,)),
            dma((E - 1,)),
            dma((C - 1,)),
            dma((C - 1,)),
        ],
        compiler_params=pltpu.CompilerParams(
            collective_id=0, has_side_effects=True, vmem_limit_bytes=60 * 1024 * 1024
        ),
        cost_estimate=pl.CostEstimate(
            flops=6 * rows * D * F, bytes_accessed=6 * D * F, transcendentals=rows * F
        ),
    )(tokens, router_weight.T, expert_ids.T, gate_weight, up_weight, down_weight)
    smem = pl.BlockSpec(memory_space=pltpu.SMEM)
    return pl.pallas_call(
        hand_on,
        out_shape=(jax.ShapeDtypeStruct((R, D), bf16), jax.ShapeDtypeStruct((2,), f32)),
        in_specs=[vmem, smem],
        out_specs=(vmem, smem),
    )(rows_out, stats)


def solution(mesh):
    placed = (
        P(("groups", "expert", "cuts"), None),
        P(),
        P("expert", None, "cuts"),
        P("expert", None, "cuts"),
        P("expert", "cuts", None),
        P(("groups", "expert", "cuts"), None),
    )
    return jax.shard_map(
        shards,
        mesh=mesh,
        in_specs=placed,
        out_specs=(P(("groups", "expert", "cuts"), None), P("groups")),
        check_vma=False,
    )
```
